32 devices in a mesh: groups: 2 (over x), ctx: 16 (over z, y, core).
Axes of the slice: x: 2, y: 2, z: 4, core: 2. Of those that a mesh axis runs over, the one named last changes fastest.
Arguments:
- xbc: bfloat16 [8192, 9216], P(('groups', 'ctx')), parts along dimension 0, may hold values from -35 to 35
- conv_carry: bfloat16 [6, 9216], P('groups'), parts along dimension 0, may hold values from -6 to 6
- conv_weight: float32 [4, 9216], replicated, may hold values from -0.9 to 0.9
- step_size: float32 [8192, 128], P(('groups', 'ctx')), parts along dimension 0, may hold values from 0.01 to 0.1
- decay: float32 [8192, 128], P(('groups', 'ctx')), parts along dimension 0, may hold values from 0.3 to 1
- skip_gain: float32 [128], replicated, may hold values from 0.5 to 1.5
- norm_gain: float32 [8192], replicated, may hold values from 0.5 to 1.5
- init_state: bfloat16 [256, 64, 128], P('groups'), parts along dimension 0, may hold values from -6 to 6
Outputs:
- mixed_out: bfloat16 [8192, 8192], P(('groups', 'ctx')), parts along dimension 0
- final_state: float32 [256, 64, 128], P(('groups', 'ctx')), parts along dimension 0
The draws below stay inside these ranges and needn't reach their ends.
There are 2 independent parts, one for each index of `groups`. The reference program is written for one: setup_inputs(seed, part) draws one part's arguments, and reference() takes and returns one part's arrays. A program takes and returns all parts, laid end to end along the dimension named above; an argument that names none is the same for every part. Nothing has to cross between parts.
All inputs are finite; a program needn't handle non-finite values.
Results may differ from the reference program's by a relative error of at most 0.0048.
Values may be sent and summed in bfloat16 or wider, within the bound.
A program may use at most 256 MiB of HBM per device.

```python
import math
import jax
import jax.numpy as jnp
from jax import lax

HEADS = 128
P_SIZE = 64
N = 128
GROUPS = 4
SPAN = 128
KW = 4
TOK_DEV = 256
WINDOW_TOKENS = 4096
INNER = 8192
CONV_CH = 9216


def draw_xbc(key, part):
    key = jax.random.fold_in(key, 1)
    random_split_keys = jax.random.split(key, 2)
    scales = jnp.exp(jax.random.uniform(random_split_keys[1], (WINDOW_TOKENS, 1), minval=0.0, maxval=math.log(10.0)))
    base_draw = jnp.clip(jax.random.normal(random_split_keys[0], (WINDOW_TOKENS, CONV_CH)), -3.5, 3.5)
    column = lax.broadcasted_iota(jnp.int32, (1, CONV_CH), 1)
    factor = jnp.where(column < HEADS * P_SIZE, scales, 1.0)
    return (base_draw * factor).astype(jnp.bfloat16)


def draw_decay(key, part):
    key = jax.random.fold_in(key, 2)
    random_split_keys = jax.random.split(key, 7)
    fast_share = 0.5
    fast_heads = jax.random.uniform(random_split_keys[0], (HEADS,)) < fast_share
    fast_rate = jnp.exp(jax.random.uniform(random_split_keys[1], (HEADS,), minval=math.log(1.0 / 50.0), maxval=math.log(1.0 / 30.0)))
    slow_rate = jnp.exp(jax.random.uniform(random_split_keys[2], (HEADS,), minval=math.log(0.05), maxval=math.log(0.5))) / WINDOW_TOKENS
    per_head_rate = jnp.where(fast_heads, fast_rate, slow_rate)
    jitter_amplitude = jnp.exp(jax.random.uniform(random_split_keys[3], (WINDOW_TOKENS, HEADS), minval=-math.log(2.0), maxval=math.log(2.0)))
    block_rate = jnp.exp(jax.random.uniform(random_split_keys[4], (WINDOW_TOKENS // TOK_DEV, HEADS), minval=-math.log(2.0), maxval=math.log(2.0)))
    rows_per_block = jnp.repeat(block_rate, TOK_DEV, axis=0)
    spike_row_list = jax.random.randint(random_split_keys[5], (2,), 0, WINDOW_TOKENS)
    spike_magnitude = jax.random.uniform(random_split_keys[6], (2,), minval=0.22, maxval=0.5)
    index_of_row = lax.broadcasted_iota(jnp.int32, (WINDOW_TOKENS, 1), 0)
    spike_event = jnp.where(index_of_row == spike_row_list[0], spike_magnitude[0], 0.0) + jnp.where(index_of_row == spike_row_list[1], spike_magnitude[1], 0.0)
    return jnp.exp(-per_head_rate[None, :] * jitter_amplitude * rows_per_block - spike_event).astype(jnp.float32)


def shard_levels(key, shape, shards, low, largest):
    def one(position, blocks):
        heights = jax.random.uniform(jax.random.fold_in(jax.random.fold_in(key, 6), position), (blocks,), jnp.float32, low / len(shards), largest / len(shards))
        return jnp.repeat(jnp.exp(heights), shape[position] // blocks).reshape((-1,) + (1,) * (len(shape) - position - 1))

    factor_of = one(*shards[0])
    for cut in shards[1:]:
        factor_of = factor_of * one(*cut)
    return factor_of


def normal_values(rng, extent, spread, bound, dtype=jnp.bfloat16):
    array = spread * jax.random.normal(rng, extent, jnp.float32)
    return jnp.clip(array, min=-bound, max=bound).astype(dtype)


def setup_inputs(seed: int = 0, part: int = 0) -> dict:
    keys = jax.random.split(jax.random.key(seed), 9)
    part_splits = jax.random.split(jax.random.fold_in(keys[8], part), 9)
    xbc = draw_xbc(jax.random.fold_in(jax.random.fold_in(keys[8], part), 71), part)
    conv_carry = normal_values(part_splits[1], (KW - 1, CONV_CH), 1.0, 6.0)
    conv_weight = normal_values(keys[2], (KW, CONV_CH), 0.15, 0.9, jnp.float32)
    step_size = jnp.clip(jnp.exp(math.log(0.1) - 2.3025851 * jax.random.uniform(part_splits[3], (WINDOW_TOKENS, HEADS), jnp.float32) ** shard_levels(part_splits[3], (WINDOW_TOKENS, HEADS), ((0, 16),), -0.2, 0.2)), 0.01, 0.1)
    decay = draw_decay(jax.random.fold_in(jax.random.fold_in(keys[8], part), 71), part)
    skip_gain = jnp.clip(jax.random.uniform(keys[5], (HEADS,), jnp.float32, 0.5, 1.5), 0.5, 1.5)
    norm_gain = jnp.clip(1.0 + 0.1 * jax.random.normal(keys[6], (INNER,), jnp.float32), 0.5, 1.5)
    init_state = normal_values(part_splits[7], (HEADS, P_SIZE, N), 1.0, 6.0)
    return {"xbc": xbc, "conv_carry": conv_carry, "conv_weight": conv_weight, "step_size": step_size, "decay": decay, "skip_gain": skip_gain, "norm_gain": norm_gain, "init_state": init_state}


def conv_silu(padded, conv_weight, row_count):
    summed = jnp.zeros((row_count, padded.shape[1]), jnp.float32)
    for offset in range(conv_weight.shape[0]):
        summed = summed + padded[offset:offset + row_count].astype(jnp.float32) * conv_weight[offset]
    return jax.nn.silu(summed).astype(jnp.bfloat16)

def inside(values_part, b_part, c_part, step_part, log_part):
    length, head_count, head_dim = values_part.shape
    groups = b_part.shape[1]
    per_group = head_count // groups
    cum_log = jnp.cumsum(log_part, axis=0)
    scores = jnp.einsum('ign,jgn->gij', c_part.astype(jnp.float32), b_part.astype(jnp.float32))
    scores = jnp.repeat(scores, per_group, axis=0)
    cum_heads = cum_log.T
    index_of_row = lax.broadcasted_iota(jnp.int32, (length, length), 0)
    col_index = lax.broadcasted_iota(jnp.int32, (length, length), 1)
    lower_mask = (index_of_row >= col_index)[None]
    log_gaps = jnp.where(lower_mask, cum_heads[:, :, None] - cum_heads[:, None, :], 0.0)
    weights = jnp.where(lower_mask, scores * jnp.exp(log_gaps) * step_part.T[:, None, :], 0.0).astype(jnp.bfloat16)
    diag_part = jnp.einsum('hij,jhp->ihp', weights.astype(jnp.float32), values_part.astype(jnp.float32))
    to_end = jnp.exp(cum_log[-1][None, :] - cum_log)
    scaled = (values_part.astype(jnp.float32) * (to_end * step_part)[:, :, None]).astype(jnp.bfloat16)
    local_state = jnp.einsum('jgkp,jgn->gkpn', scaled.reshape(length, groups, per_group, head_dim).astype(jnp.float32), b_part.astype(jnp.float32))
    return (diag_part, local_state.reshape(head_count, head_dim, b_part.shape[2]), cum_log)

def carried(carry_state, c_part, cum_log):
    head_count, head_dim, state_dim = carry_state.shape
    groups = c_part.shape[1]
    grouped = carry_state.reshape(groups, head_count // groups, head_dim, state_dim)
    off_part = jnp.einsum('gkpn,ign->igkp', grouped, c_part.astype(jnp.float32), precision=lax.Precision.HIGHEST)
    return off_part.reshape(c_part.shape[0], head_count, head_dim) * jnp.exp(cum_log)[:, :, None]

def finish(diag_part, off_part, values_part, skip_gain, norm_gain, groups):
    summed = diag_part + off_part + skip_gain[None, :, None] * values_part.astype(jnp.float32)
    length = summed.shape[0]
    grouped = summed.reshape(length, groups, -1)
    factor = lax.rsqrt(lax.optimization_barrier(jnp.mean(grouped * grouped, axis=-1, keepdims=True)) + 1e-05)
    return ((grouped * factor).reshape(length, -1) * norm_gain[None, :]).astype(jnp.bfloat16)

def reference(xbc, conv_carry, conv_weight, step_size, decay, skip_gain, norm_gain, init_state):
    padded = jnp.concatenate([conv_carry, xbc], axis=0)
    activated = conv_silu(padded, conv_weight, WINDOW_TOKENS)
    inner_width = HEADS * P_SIZE
    blocks = WINDOW_TOKENS // SPAN
    values_all = activated[:, :inner_width].reshape(blocks, SPAN, HEADS, P_SIZE)
    b_all = activated[:, inner_width:inner_width + GROUPS * N].reshape(blocks, SPAN, GROUPS, N)
    c_all = activated[:, inner_width + GROUPS * N:].reshape(blocks, SPAN, GROUPS, N)
    steps_all = step_size.reshape(blocks, SPAN, HEADS)
    logs_all = jnp.log(decay).reshape(blocks, SPAN, HEADS)

    def advance(carry_state, pieces):
        values_part, b_part, c_part, step_part, log_part = pieces
        diag_part, local_state, cum_log = inside(values_part, b_part, c_part, step_part, log_part)
        off_part = carried(carry_state, c_part, cum_log)
        out_rows = finish(diag_part, off_part, values_part, skip_gain, norm_gain, GROUPS)
        new_state = jnp.exp(cum_log[-1])[:, None, None] * carry_state + local_state
        return (new_state, out_rows)
    final_state, outputs = lax.scan(advance, init_state.astype(jnp.float32), (values_all, b_all, c_all, steps_all, logs_all))
    return (outputs.reshape(WINDOW_TOKENS, inner_width), final_state)
```

```python
import jax
import jax.numpy as jnp
from jax import lax
from jax.experimental import pallas as pl
from jax.experimental.pallas import tpu as pltpu
from jax.sharding import PartitionSpec as P

P_SIZE = 64
N = 128
GROUPS = 4
LANES = 128
F32 = jnp.float32
BF16 = jnp.bfloat16
VMEM_LIMIT = 48 * 1024 * 1024


def params():
    return pltpu.CompilerParams(
        dimension_semantics=("arbitrary",), vmem_limit_bytes=VMEM_LIMIT
    )


def split_bf16(value):
    high = value.astype(BF16)
    low = (value - high.astype(F32)).astype(BF16)
    return high, low


def conv_columns(x_ref, early_ref, weight_ref, out_ref, padded, rows):
    def column(index, _):
        at = pl.ds(pl.multiple_of(index * LANES, LANES), LANES)
        padded[0:8, :] = early_ref[:, at]
        padded[8 : 8 + rows, :] = x_ref[:, at].astype(F32)
        taps = weight_ref[:, at]
        summed = taps[0:1] * padded[5 : 5 + rows, :]
        for tap in range(1, 4):
            summed = summed + taps[tap : tap + 1] * padded[5 + tap : 5 + tap + rows, :]
        half = 0.5 * summed
        out_ref[:, at] = (half * jnp.tanh(half) + half).astype(BF16)
        return 0

    lax.fori_loop(0, x_ref.shape[1] // LANES, column, 0)


def conv_kernel(
    xv, xb, xc, ev, eb, ec, wv, wb, wc, factor, expand, act_v, act_b, act_c, state, padded
):
    rows = xv.shape[0]
    conv_columns(xv, ev, wv, act_v, padded, rows)
    conv_columns(xb, eb, wb, act_b, padded, rows)
    conv_columns(xc, ec, wc, act_c, padded, rows)
    b_turned = act_b[...].astype(F32).T.astype(BF16)
    dests, _, share = state.shape
    for dest in range(dests):
        at = slice(dest * share, (dest + 1) * share)
        wide = jnp.dot(factor[0], expand[:, at], preferred_element_type=F32)
        scaled = (act_v[:, at].astype(F32) * wide).astype(BF16)
        state[dest] = jnp.dot(b_turned, scaled, preferred_element_type=F32).astype(BF16)


def diag_kernel(act_v, act_b, act_c, cum_rows, shifted, skip, partial):
    rows = act_v.shape[0]
    half = rows // 2
    heads = cum_rows.shape[2]
    scores = lax.dot_general(
        act_c[...], act_b[...], (((1,), (1,)), ((), ())), preferred_element_type=F32
    )
    row_index = lax.broadcasted_iota(jnp.int32, (half, half), 0)
    col_index = lax.broadcasted_iota(jnp.int32, (half, half), 1)
    lower = row_index >= col_index
    first_lanes = lax.broadcasted_iota(jnp.int32, (half, 2 * P_SIZE), 1) < P_SIZE
    cum = cum_rows[0]
    for pair in range(heads // 2):
        at = slice(pair * 2 * P_SIZE, (pair + 1) * 2 * P_SIZE)
        values = act_v[:, at]
        tops, lows = [], []
        for head in (2 * pair, 2 * pair + 1):
            own = cum[:, head : head + 1]
            other = shifted[head : head + 1, :]
            top = jnp.where(lower, own[:half] - other[:, :half], -1e30)
            w_top = (scores[:half, :half] * jnp.exp2(top)).astype(BF16)
            left = own[half:] - other[:, :half]
            w_left = (scores[half:, :half] * jnp.exp2(left)).astype(BF16)
            right = jnp.where(lower, own[half:] - other[:, half:], -1e30)
            w_right = (scores[half:, half:] * jnp.exp2(right)).astype(BF16)
            tops.append(jnp.dot(w_top, values[:half], preferred_element_type=F32))
            w_low = jnp.concatenate([w_left, w_right], axis=1)
            lows.append(jnp.dot(w_low, values, preferred_element_type=F32))
        gain = skip[:, at]
        wide = values.astype(F32)
        partial[:half, at] = (
            jnp.where(first_lanes, tops[0], tops[1]) + gain * wide[:half]
        ).astype(BF16)
        partial[half:, at] = (
            jnp.where(first_lanes, lows[0], lows[1]) + gain * wide[half:]
        ).astype(BF16)


def chain_kernel(states, decays, start, entering, final):
    def step(index, now):
        entering[index] = now.astype(BF16)
        return decays[index] * now + states[index].astype(F32)

    final[...] = lax.fori_loop(0, states.shape[0], step, start[...])


def finish_kernel(partial, act_c, incoming, grown, expand, gain, out, summed):
    dests, _, share = incoming.shape
    squares = jnp.zeros((partial.shape[0], 1), F32)
    for dest in range(dests):
        at = slice(dest * share, (dest + 1) * share)
        wide = jnp.dot(grown[0], expand[:, at], preferred_element_type=F32)
        off = jnp.dot(act_c[...], incoming[dest], preferred_element_type=F32)
        total = partial[:, at].astype(F32) + wide * off
        summed[:, at] = total
        squares = squares + jnp.sum(total * total, axis=1, keepdims=True)
    factor = lax.rsqrt(squares * (1.0 / out.shape[1]) + 1e-05)
    for dest in range(dests):
        at = slice(dest * share, (dest + 1) * share)
        out[:, at] = (summed[:, at] * factor * gain[:, at]).astype(BF16)


def shards(xbc, conv_carry, conv_weight, step_size, decay, skip_gain, norm_gain, init_state):
    taps, channels = conv_weight.shape
    rows = xbc.shape[0]
    heads = step_size.shape[1]
    inner = heads * P_SIZE
    count = lax.axis_size("ctx")
    position = lax.axis_index("ctx")
    share = inner // count
    head_share = heads // count
    width = inner // GROUPS
    per_group = heads // GROUPS
    dests = width // share

    edge = xbc[rows - (taps - 1) :]
    received = lax.ppermute(edge, "ctx", [(s, s + 1) for s in range(count - 1)])
    earlier = jnp.where(position == 0, conv_carry, received).astype(F32)
    earlier = jnp.pad(earlier, ((8 - (taps - 1), 0), (0, 0)))

    logs = jnp.log2(decay)
    lower = jnp.tril(jnp.ones((rows, rows), F32))
    cum = jnp.dot(lower, logs, precision=lax.Precision.HIGHEST)
    total = cum[-1]

    def by_group(value):
        return value.reshape(rows, GROUPS, -1).transpose(1, 0, 2)

    def doubled(value):
        high, low = split_bf16(by_group(value))
        return jnp.concatenate([high, low], axis=2)

    factor = doubled(jnp.exp2(total - cum) * step_size)
    grown = doubled(jnp.exp2(cum))
    shifted = (cum - jnp.log2(step_size)).T
    spread = jnp.repeat(jnp.eye(per_group, dtype=BF16), P_SIZE, axis=1)
    expand = jnp.concatenate([spread, spread], axis=0)

    totals = lax.all_to_all(
        total.reshape(count, head_share), "ctx", split_axis=0, concat_axis=0, tiled=True
    )
    decays = jnp.repeat(jnp.exp2(totals), P_SIZE, axis=1)[:, None, :]

    def wide(height):
        return pl.BlockSpec((height, width), lambda g: (0, g))

    def thin(height, first):
        return pl.BlockSpec((height, N), lambda g: (0, first + g))

    def per(*shape):
        return pl.BlockSpec((1,) + shape, lambda g: (g, 0, 0))

    whole_expand = pl.BlockSpec((2 * per_group, width), lambda g: (0, 0))
    piece = pl.BlockSpec((dests, N, share), lambda g: (g, 0, 0))
    b_first, c_first = inner // N, inner // N + GROUPS
    act_v, act_b, act_c, own = pl.pallas_call(
        conv_kernel,
        grid=(GROUPS,),
        in_specs=[
            wide(rows), thin(rows, b_first), thin(rows, c_first),
            wide(8), thin(8, b_first), thin(8, c_first),
            wide(taps), thin(taps, b_first), thin(taps, c_first),
            per(rows, 2 * per_group), whole_expand,
        ],
        out_specs=[wide(rows), thin(rows, 0), thin(rows, 0), piece],
        out_shape=[
            jax.ShapeDtypeStruct((rows, inner), BF16),
            jax.ShapeDtypeStruct((rows, GROUPS * N), BF16),
            jax.ShapeDtypeStruct((rows, GROUPS * N), BF16),
            jax.ShapeDtypeStruct((count, N, share), BF16),
        ],
        scratch_shapes=[pltpu.VMEM((8 + rows, LANES), F32)],
        compiler_params=params(),
        name="conv_state",
    )(xbc, xbc, xbc, earlier, earlier, earlier, conv_weight, conv_weight, conv_weight, factor, expand)

    states = lax.all_to_all(own, "ctx", split_axis=0, concat_axis=0, tiled=True)

    partial = pl.pallas_call(
        diag_kernel,
        grid=(GROUPS,),
        in_specs=[
            wide(rows), thin(rows, 0), thin(rows, 0), per(rows, per_group),
            pl.BlockSpec((per_group, rows), lambda g: (g, 0)), wide(1),
        ],
        out_specs=wide(rows),
        out_shape=jax.ShapeDtypeStruct((rows, inner), BF16),
        compiler_params=params(),
        cost_estimate=pl.CostEstimate(
            flops=heads * rows * rows * P_SIZE * 16,
            bytes_accessed=rows * inner * 4,
            transcendentals=heads * rows * rows,
        ),
        name="diag",
    )(act_v, act_b, act_c, by_group(cum), shifted, jnp.repeat(skip_gain, P_SIZE)[None])

    start = lax.dynamic_slice_in_dim(init_state, position * head_share, head_share, 0)
    start = start.astype(F32).reshape(share, N).T
    entering, final = pl.pallas_call(
        chain_kernel,
        grid=(share // LANES,),
        in_specs=[
            pl.BlockSpec((count, N, LANES), lambda i: (0, 0, i)),
            pl.BlockSpec((count, 1, LANES), lambda i: (0, 0, i)),
            pl.BlockSpec((N, LANES), lambda i: (0, i)),
        ],
        out_specs=[
            pl.BlockSpec((count, N, LANES), lambda i: (0, 0, i)),
            pl.BlockSpec((N, LANES), lambda i: (0, i)),
        ],
        out_shape=[
            jax.ShapeDtypeStruct((count, N, share), BF16),
            jax.ShapeDtypeStruct((N, share), F32),
        ],
        compiler_params=params(),
        name="chain",
    )(states, decays, start)
    final_state = final.T.reshape(head_share, P_SIZE, N)

    incoming = lax.all_to_all(entering, "ctx", split_axis=0, concat_axis=0, tiled=True)

    mixed_out = pl.pallas_call(
        finish_kernel,
        grid=(GROUPS,),
        in_specs=[
            wide(rows), thin(rows, 0), piece, per(rows, 2 * per_group), whole_expand, wide(1),
        ],
        out_specs=wide(rows),
        out_shape=jax.ShapeDtypeStruct((rows, inner), BF16),
        scratch_shapes=[pltpu.VMEM((rows, width), F32)],
        compiler_params=params(),
        name="finish",
    )(partial, act_c, incoming, grown, expand, norm_gain[None])
    return (mixed_out, final_state)


def solution(mesh):
    return jax.shard_map(
        shards,
        mesh=mesh,
        in_specs=(
            P(("groups", "ctx"), None),
            P("groups", None),
            P(),
            P(("groups", "ctx"), None),
            P(("groups", "ctx"), None),
            P(),
            P(),
            P("groups", None, None),
        ),
        out_specs=(P(("groups", "ctx"), None), P(("groups", "ctx"), None, None)),
        check_vma=False,
    )
```

```python
import functools

import jax
import jax.numpy as jnp
from jax import lax
from jax.experimental import pallas as pl
from jax.experimental.pallas import tpu as pltpu
from jax.sharding import PartitionSpec as P

P_SIZE = 64
N = 128
GROUPS = 4
LANES = 128
F32 = jnp.float32
BF16 = jnp.bfloat16
VMEM_LIMIT = 48 * 1024 * 1024


def params():
    return pltpu.CompilerParams(
        dimension_semantics=("arbitrary",), vmem_limit_bytes=VMEM_LIMIT
    )


def split_bf16(value):
    high = value.astype(BF16)
    low = (value - high.astype(F32)).astype(BF16)
    return high, low


def conv_columns(x_ref, early_ref, weight_ref, out_ref, padded, rows):
    def column(index, _):
        at = pl.ds(pl.multiple_of(index * LANES, LANES), LANES)
        padded[0:8, :] = early_ref[:, at]
        padded[8 : 8 + rows, :] = x_ref[:, at].astype(F32)
        taps = weight_ref[:, at]
        summed = taps[0:1] * padded[5 : 5 + rows, :]
        for tap in range(1, 4):
            summed = summed + taps[tap : tap + 1] * padded[5 + tap : 5 + tap + rows, :]
        half = 0.5 * summed
        out_ref[:, at] = (half * jnp.tanh(half) + half).astype(BF16)
        return 0

    lax.fori_loop(0, x_ref.shape[1] // LANES, column, 0)


def conv_kernel(
    xv, xb, xc, ev, eb, ec, wv, wb, wc, factor, expand, act_v, act_b, act_c, state, padded
):
    rows = xv.shape[0]
    conv_columns(xv, ev, wv, act_v, padded, rows)
    conv_columns(xb, eb, wb, act_b, padded, rows)
    conv_columns(xc, ec, wc, act_c, padded, rows)
    b_turned = act_b[...].astype(F32).T.astype(BF16)
    share = state.shape[-1]
    dests = xv.shape[1] // share
    for dest in range(dests):
        at = slice(dest * share, (dest + 1) * share)
        wide = jnp.dot(factor[0], expand[:, at], preferred_element_type=F32)
        scaled = (act_v[:, at].astype(F32) * wide).astype(BF16)
        state[dest % 2, dest // 2 % 2, dest // 4] = jnp.dot(b_turned, scaled, preferred_element_type=F32).astype(BF16)


def diag_kernel(act_v, act_b, act_c, cum_rows, shifted, skip, partial):
    rows = act_v.shape[0]
    half = rows // 2
    heads = cum_rows.shape[2]
    scores = lax.dot_general(
        act_c[...], act_b[...], (((1,), (1,)), ((), ())), preferred_element_type=F32
    )
    row_index = lax.broadcasted_iota(jnp.int32, (half, half), 0)
    col_index = lax.broadcasted_iota(jnp.int32, (half, half), 1)
    lower = row_index >= col_index
    first_lanes = lax.broadcasted_iota(jnp.int32, (half, 2 * P_SIZE), 1) < P_SIZE
    cum = cum_rows[0]
    for pair in range(heads // 2):
        at = slice(pair * 2 * P_SIZE, (pair + 1) * 2 * P_SIZE)
        values = act_v[:, at]
        tops, lows = [], []
        for head in (2 * pair, 2 * pair + 1):
            own = cum[:, head : head + 1]
            other = shifted[head : head + 1, :]
            top = jnp.where(lower, own[:half] - other[:, :half], -1e30)
            w_top = (scores[:half, :half] * jnp.exp2(top)).astype(BF16)
            left = own[half:] - other[:, :half]
            w_left = (scores[half:, :half] * jnp.exp2(left)).astype(BF16)
            right = jnp.where(lower, own[half:] - other[:, half:], -1e30)
            w_right = (scores[half:, half:] * jnp.exp2(right)).astype(BF16)
            tops.append(jnp.dot(w_top, values[:half], preferred_element_type=F32))
            w_low = jnp.concatenate([w_left, w_right], axis=1)
            lows.append(jnp.dot(w_low, values, preferred_element_type=F32))
        gain = skip[:, at]
        wide = values.astype(F32)
        partial[:half, at] = (
            jnp.where(first_lanes, tops[0], tops[1]) + gain * wide[:half]
        ).astype(BF16)
        partial[half:, at] = (
            jnp.where(first_lanes, lows[0], lows[1]) + gain * wide[half:]
        ).astype(BF16)


def scan_kernel(
    planes, own, decays, start, incoming, final,
    cores, sent, kept, chips, plane_out, plane_in, enter, entered, back, mixed, handed,
    core_send, core_recv, chip_send, chip_recv, out_send, out_recv,
    in_send, in_recv, back_send, back_recv, hand_send, hand_recv,
):
    position = lax.axis_index("ctx")
    z, y, c = position // 4, (position // 2) % 2, position % 2
    core_peer = position + 1 - 2 * c
    chip_peer = position + 2 - 4 * y
    away = [(z + step) % planes for step in range(planes)]
    order = list(range(1, planes)) + [0]
    first_core = c == 0
    first_chip = y == 0

    def copy(source, target, send, recv, device):
        return pltpu.make_async_remote_copy(
            src_ref=source, dst_ref=target, send_sem=send, recv_sem=recv,
            device_id={"ctx": device}, device_id_type=pl.DeviceIdType.MESH,
        )

    barrier = pltpu.get_barrier_semaphore()
    friends = [core_peer, chip_peer] + [away[step] * 4 + y * 2 + c for step in range(1, planes)]
    for friend in friends:
        pl.semaphore_signal(
            barrier, inc=1, device_id={"ctx": friend}, device_id_type=pl.DeviceIdType.MESH
        )
    pl.semaphore_wait(barrier, len(friends))

    pending = []
    sides = (1 - y, y)
    swaps = []
    for turn, side in enumerate(sides):
        swap = copy(
            own.at[1 - c, side], cores.at[side], core_send.at[turn], core_recv.at[turn], core_peer
        )
        swap.start()
        swaps.append(swap)
    pending += swaps

    def core_states(side, plane):
        here, there = own[c, side, plane].astype(F32), cores[side, plane].astype(F32)
        return jnp.where(first_core, here, there), jnp.where(first_core, there, here)

    def chip_state(side, plane):
        earlier, later = core_states(side, plane)
        return decays[side * planes + plane] * earlier + later

    swaps[0].wait_recv()
    chip_copies = {}
    for step in order:
        plane = away[step]
        sent[plane] = chip_state(1 - y, plane).astype(BF16)
        chip_copies[step] = copy(
            sent.at[plane], chips.at[plane], chip_send.at[step], chip_recv.at[step], chip_peer
        )
        chip_copies[step].start()
        pending.append(chip_copies[step])
    swaps[1].wait_recv()
    for step in order:
        kept[away[step]] = chip_state(y, away[step]).astype(BF16)

    def chip_states(plane):
        here, there = kept[plane].astype(F32), chips[plane].astype(F32)
        return jnp.where(first_chip, here, there), jnp.where(first_chip, there, here)

    out_copies = {}
    for step in order:
        plane = away[step]
        chip_copies[step].wait_recv()
        earlier, later = chip_states(plane)
        both = (decays[4 * planes + plane] * earlier + later).astype(BF16)
        if step == 0:
            plane_in[plane] = both
        else:
            plane_out[plane] = both
            out_copies[step] = copy(
                plane_out.at[plane], plane_in.at[z], out_send.at[step], out_recv.at[step],
                plane * 4 + y * 2 + c,
            )
            out_copies[step].start()
            pending.append(out_copies[step])
    for step in range(1, planes):
        out_copies[step].wait_recv()

    now = start[...]
    for plane in range(planes):
        enter[plane] = now.astype(BF16)
        now = decays[6 * planes + plane] * now + plane_in[plane].astype(F32)
    final[...] = now
    in_copies = {}
    for step in range(1, planes):
        plane = away[step]
        in_copies[step] = copy(
            enter.at[plane], entered.at[z], in_send.at[step], in_recv.at[step],
            plane * 4 + y * 2 + c,
        )
        in_copies[step].start()
        pending.append(in_copies[step])

    hands = []

    def to_cores(side, plane, state, slot):
        earlier, _ = core_states(side, plane)
        later = decays[2 * planes + side * planes + plane] * state + earlier
        incoming[c, side, plane] = jnp.where(first_core, state, later).astype(BF16)
        handed[side, plane] = jnp.where(first_core, later, state).astype(BF16)
        hand = copy(
            handed.at[side, plane], incoming.at[c, side, plane],
            hand_send.at[slot], hand_recv.at[slot], core_peer,
        )
        hand.start()
        hands.append(hand)

    back_copies = {}
    receive_order = [0] + list(range(1, planes))
    for step in receive_order:
        plane = (z + planes - step) % planes
        if step == 0:
            state = enter[plane].astype(F32)
        else:
            in_copies[step].wait_recv()
            state = entered[plane].astype(F32)
        earlier, _ = chip_states(plane)
        later = decays[5 * planes + plane] * state + earlier
        back[plane] = jnp.where(first_chip, later, state).astype(BF16)
        back_copies[step] = copy(
            back.at[plane], mixed.at[plane], back_send.at[step], back_recv.at[step], chip_peer
        )
        back_copies[step].start()
        pending.append(back_copies[step])
        to_cores(y, plane, jnp.where(first_chip, state, later), step)
    for step in receive_order:
        plane = (z + planes - step) % planes
        back_copies[step].wait_recv()
        to_cores(1 - y, plane, mixed[plane].astype(F32), planes + step)
    for hand in hands:
        hand.wait_recv()
    for item in pending + hands:
        item.wait_send()


def finish_kernel(partial, act_c, incoming, grown, expand, gain, out, summed):
    share = incoming.shape[-1]
    dests = out.shape[1] // share
    squares = jnp.zeros((partial.shape[0], 1), F32)
    for dest in range(dests):
        at = slice(dest * share, (dest + 1) * share)
        wide = jnp.dot(grown[0], expand[:, at], preferred_element_type=F32)
        off = jnp.dot(
            act_c[...], incoming[dest % 2, dest // 2 % 2, dest // 4], preferred_element_type=F32
        )
        total = partial[:, at].astype(F32) + wide * off
        summed[:, at] = total
        squares = squares + jnp.sum(total * total, axis=1, keepdims=True)
    factor = lax.rsqrt(squares * (1.0 / out.shape[1]) + 1e-05)
    for dest in range(dests):
        at = slice(dest * share, (dest + 1) * share)
        out[:, at] = (summed[:, at] * factor * gain[:, at]).astype(BF16)


def shards(xbc, conv_carry, conv_weight, step_size, decay, skip_gain, norm_gain, init_state):
    taps, channels = conv_weight.shape
    rows = xbc.shape[0]
    heads = step_size.shape[1]
    inner = heads * P_SIZE
    count = lax.axis_size("ctx")
    position = lax.axis_index("ctx")
    share = inner // count
    head_share = heads // count
    width = inner // GROUPS
    per_group = heads // GROUPS
    dests = width // share

    edge = xbc[rows - (taps - 1) :]
    received = lax.ppermute(edge, "ctx", [(s, s + 1) for s in range(count - 1)])
    earlier = jnp.where(position == 0, conv_carry, received).astype(F32)
    earlier = jnp.pad(earlier, ((8 - (taps - 1), 0), (0, 0)))

    logs = jnp.log2(decay)
    lower = jnp.tril(jnp.ones((rows, rows), F32))
    cum = jnp.dot(lower, logs, precision=lax.Precision.HIGHEST)
    total = cum[-1]

    def by_group(value):
        return value.reshape(rows, GROUPS, -1).transpose(1, 0, 2)

    def doubled(value):
        high, low = split_bf16(by_group(value))
        return jnp.concatenate([high, low], axis=2)

    factor = doubled(jnp.exp2(total - cum) * step_size)
    grown = doubled(jnp.exp2(cum))
    shifted = (cum - jnp.log2(step_size)).T
    spread = jnp.repeat(jnp.eye(per_group, dtype=BF16), P_SIZE, axis=1)
    expand = jnp.concatenate([spread, spread], axis=0)

    planes = count // 4
    at_z, at_y, at_c = position // 4, (position // 2) % 2, position % 2
    every = lax.all_gather(total, "ctx").reshape(planes, 2, 2, planes, 2, 2, head_share)
    every = every[:, :, :, :, :, at_c].transpose(0, 1, 2, 4, 3, 5)
    plane_now = every[at_z]
    pieces = [
        plane_now[at_y, 1].reshape(2 * planes, head_share),
        plane_now[at_y, 0].reshape(2 * planes, head_share),
        plane_now[1].sum(0)[at_y],
        plane_now[0].sum(0)[at_y],
        every.sum((1, 2))[:, at_y, at_z],
    ]
    decays = jnp.repeat(jnp.exp2(jnp.concatenate(pieces, axis=0)), P_SIZE, axis=1)[:, None, :]

    def wide(height):
        return pl.BlockSpec((height, width), lambda g: (0, g))

    def thin(height, first):
        return pl.BlockSpec((height, N), lambda g: (0, first + g))

    def per(*shape):
        return pl.BlockSpec((1,) + shape, lambda g: (g, 0, 0))

    whole_expand = pl.BlockSpec((2 * per_group, width), lambda g: (0, 0))
    piece = pl.BlockSpec((2, 2, dests // 4, N, share), lambda g: (0, 0, g, 0, 0))
    b_first, c_first = inner // N, inner // N + GROUPS
    act_v, act_b, act_c, own = pl.pallas_call(
        conv_kernel,
        grid=(GROUPS,),
        in_specs=[
            wide(rows), thin(rows, b_first), thin(rows, c_first),
            wide(8), thin(8, b_first), thin(8, c_first),
            wide(taps), thin(taps, b_first), thin(taps, c_first),
            per(rows, 2 * per_group), whole_expand,
        ],
        out_specs=[wide(rows), thin(rows, 0), thin(rows, 0), piece],
        out_shape=[
            jax.ShapeDtypeStruct((rows, inner), BF16),
            jax.ShapeDtypeStruct((rows, GROUPS * N), BF16),
            jax.ShapeDtypeStruct((rows, GROUPS * N), BF16),
            jax.ShapeDtypeStruct((2, 2, planes, N, share), BF16),
        ],
        scratch_shapes=[pltpu.VMEM((8 + rows, LANES), F32)],
        compiler_params=params(),
        name="conv_state",
    )(xbc, xbc, xbc, earlier, earlier, earlier, conv_weight, conv_weight, conv_weight, factor, expand)

    partial = pl.pallas_call(
        diag_kernel,
        grid=(GROUPS,),
        in_specs=[
            wide(rows), thin(rows, 0), thin(rows, 0), per(rows, per_group),
            pl.BlockSpec((per_group, rows), lambda g: (g, 0)), wide(1),
        ],
        out_specs=wide(rows),
        out_shape=jax.ShapeDtypeStruct((rows, inner), BF16),
        compiler_params=params(),
        cost_estimate=pl.CostEstimate(
            flops=heads * rows * rows * P_SIZE * 16,
            bytes_accessed=rows * inner * 4,
            transcendentals=heads * rows * rows,
        ),
        name="diag",
    )(act_v, act_b, act_c, by_group(cum), shifted, jnp.repeat(skip_gain, P_SIZE)[None])

    start = lax.dynamic_slice_in_dim(init_state, position * head_share, head_share, 0)
    start = start.astype(F32).reshape(share, N).T
    vmem = pl.BlockSpec(memory_space=pltpu.VMEM)
    line = pltpu.VMEM((planes, N, share), BF16)
    square = pltpu.VMEM((2, planes, N, share), BF16)
    turns = pltpu.SemaphoreType.DMA((planes,))
    incoming, final = pl.pallas_call(
        functools.partial(scan_kernel, planes),
        in_specs=[vmem] * 3,
        out_specs=[vmem] * 2,
        out_shape=[
            jax.ShapeDtypeStruct((2, 2, planes, N, share), BF16),
            jax.ShapeDtypeStruct((N, share), F32),
        ],
        scratch_shapes=[square] + [line] * 9 + [square]
        + [pltpu.SemaphoreType.DMA((2,))] * 2 + [turns] * 8
        + [pltpu.SemaphoreType.DMA((2 * planes,))] * 2,
        compiler_params=pltpu.CompilerParams(
            collective_id=0, has_side_effects=True, vmem_limit_bytes=VMEM_LIMIT
        ),
        name="scan_devices",
    )(own, decays, start)
    final_state = final.T.reshape(head_share, P_SIZE, N)

    mixed_out = pl.pallas_call(
        finish_kernel,
        grid=(GROUPS,),
        in_specs=[
            wide(rows), thin(rows, 0), piece, per(rows, 2 * per_group), whole_expand, wide(1),
        ],
        out_specs=wide(rows),
        out_shape=jax.ShapeDtypeStruct((rows, inner), BF16),
        scratch_shapes=[pltpu.VMEM((rows, width), F32)],
        compiler_params=params(),
        name="finish",
    )(partial, act_c, incoming, grown, expand, norm_gain[None])
    return (mixed_out, final_state)


def solution(mesh):
    return jax.shard_map(
        shards,
        mesh=mesh,
        in_specs=(
            P(("groups", "ctx"), None),
            P("groups", None),
            P(),
            P(("groups", "ctx"), None),
            P(("groups", "ctx"), None),
            P(),
            P(),
            P("groups", None, None),
        ),
        out_specs=(P(("groups", "ctx"), None), P(("groups", "ctx"), None, None)),
        check_vma=False,
    )
```

```python
import functools

import jax
import jax.numpy as jnp
import numpy as np
from jax import lax
from jax.experimental import pallas as pl
from jax.experimental.pallas import tpu as pltpu
from jax.sharding import PartitionSpec as P

P_SIZE = 64
N = 128
GROUPS = 4
LANES = 128
F32 = jnp.float32
BF16 = jnp.bfloat16
VMEM_LIMIT = 48 * 1024 * 1024


def params():
    return pltpu.CompilerParams(
        dimension_semantics=("arbitrary",), vmem_limit_bytes=VMEM_LIMIT
    )


def split_bf16(value):
    high = value.astype(BF16)
    low = (value - high.astype(F32)).astype(BF16)
    return high, low


def prepare_kernel(decay, step, skip, factor, grown, cum_rows, shifted, skips):
    rows, heads = decay.shape
    row_index = lax.broadcasted_iota(jnp.int32, (rows, rows), 0)
    col_index = lax.broadcasted_iota(jnp.int32, (rows, rows), 1)
    lower = jnp.where(row_index >= col_index, 1.0, 0.0).astype(F32)
    cum = jnp.dot(
        lower, jnp.log2(decay[...]), precision=lax.Precision.HIGHEST, preferred_element_type=F32
    )
    shifted[...] = (cum - jnp.log2(step[...])).T
    per_group = heads // GROUPS

    def doubled(value, out):
        high, low = split_bf16(value)
        for group in range(GROUPS):
            at = slice(group * per_group, (group + 1) * per_group)
            out[group] = jnp.concatenate([high[:, at], low[:, at]], axis=1)

    doubled(jnp.exp2(cum[rows - 1 :] - cum) * step[...], factor)
    doubled(jnp.exp2(cum), grown)
    doubled(jnp.broadcast_to(skip[...], (16, heads)), skips)
    for group in range(GROUPS):
        cum_rows[group] = cum[:, group * per_group : (group + 1) * per_group]


def conv_columns(x_ref, early_ref, weight_ref, out_ref, padded, rows):
    def column(index, _):
        at = pl.ds(pl.multiple_of(index * LANES, LANES), LANES)
        padded[0:8, :] = early_ref[:, at]
        padded[8 : 8 + rows, :] = x_ref[:, at].astype(F32)
        taps = weight_ref[:, at]
        summed = taps[0:1] * padded[5 : 5 + rows, :]
        for tap in range(1, 4):
            summed = summed + taps[tap : tap + 1] * padded[5 + tap : 5 + tap + rows, :]
        half = 0.5 * summed
        out_ref[:, at] = (half * jnp.tanh(half) + half).astype(BF16)
        return 0

    lax.fori_loop(0, x_ref.shape[1] // LANES, column, 0)


def conv_kernel(
    xv, xb, xc, ev, eb, ec, wv, wb, wc, factor, grown, cum_rows, shifted, skips, expand,
    act_c, state, decays, partial, padded, act_v, act_b
):
    rows = xv.shape[0]
    conv_columns(xv, ev, wv, act_v, padded, rows)
    conv_columns(xb, eb, wb, act_b, padded, rows)
    conv_columns(xc, ec, wc, act_c, padded, rows)
    b_turned = act_b[...].astype(F32).T.astype(BF16)
    share = state.shape[-1]
    dests = xv.shape[1] // share
    for dest in range(dests):
        at = slice(dest * share, (dest + 1) * share)
        wide = jnp.dot(factor[0], expand[:, at], preferred_element_type=F32)
        scaled = (act_v[:, at].astype(F32) * wide).astype(BF16)
        state[dest % 2, dest // 2 % 2, dest // 4] = jnp.dot(b_turned, scaled, preferred_element_type=F32).astype(BF16)
        lasting = jnp.dot(grown[0, rows - 16 :], expand[:, at], preferred_element_type=F32)
        decays[dest % 2, dest // 2 % 2, dest // 4] = lasting[15:16]
    diag_part(act_v, act_b, act_c, cum_rows, shifted, skips, expand, partial)


def diag_part(act_v, act_b, act_c, cum_rows, shifted, skips, expand, partial):
    rows = act_v.shape[0]
    half = rows // 2
    heads = cum_rows.shape[2]
    scores = lax.dot_general(
        act_c[...], act_b[...], (((1,), (1,)), ((), ())), preferred_element_type=F32
    )
    row_index = lax.broadcasted_iota(jnp.int32, (half, half), 0)
    col_index = lax.broadcasted_iota(jnp.int32, (half, half), 1)
    lower = row_index >= col_index
    first_lanes = lax.broadcasted_iota(jnp.int32, (half, 2 * P_SIZE), 1) < P_SIZE
    cum = cum_rows[0]
    for pair in range(heads // 2):
        at = slice(pair * 2 * P_SIZE, (pair + 1) * 2 * P_SIZE)
        values = act_v[:, at]
        tops, lows = [], []
        for head in (2 * pair, 2 * pair + 1):
            own = cum[:, head : head + 1]
            other = shifted[head : head + 1, :]
            top = jnp.where(lower, own[:half] - other[:, :half], -1e30)
            w_top = (scores[:half, :half] * jnp.exp2(top)).astype(BF16)
            left = own[half:] - other[:, :half]
            w_left = (scores[half:, :half] * jnp.exp2(left)).astype(BF16)
            right = jnp.where(lower, own[half:] - other[:, half:], -1e30)
            w_right = (scores[half:, half:] * jnp.exp2(right)).astype(BF16)
            tops.append(jnp.dot(w_top, values[:half], preferred_element_type=F32))
            w_low = jnp.concatenate([w_left, w_right], axis=1)
            lows.append(jnp.dot(w_low, values, preferred_element_type=F32))
        gain = jnp.dot(skips[0], expand[:, at], preferred_element_type=F32)[0:1]
        wide = values.astype(F32)
        partial[:half, at] = (
            jnp.where(first_lanes, tops[0], tops[1]) + gain * wide[:half]
        ).astype(BF16)
        partial[half:, at] = (
            jnp.where(first_lanes, lows[0], lows[1]) + gain * wide[half:]
        ).astype(BF16)


def scan_kernel(
    planes, own, decays, start, incoming, final,
    cores, sent, kept, chips, plane_out, plane_in, enter, entered, back, mixed, handed,
    core_rates, chip_rate_out, chip_rates, plane_rate_out, plane_rates,
    core_send, core_recv, chip_send, chip_recv, out_send, out_recv,
    in_send, in_recv, back_send, back_recv, rate_send, rate_recv,
    hand_send, hand_recv, few_send, few_recv,
):
    position = lax.axis_index("ctx")
    z, y, c = position // 4, (position // 2) % 2, position % 2
    core_peer = position + 1 - 2 * c
    chip_peer = position + 2 - 4 * y
    away = [(z + step) % planes for step in range(planes)]
    order = list(range(1, planes)) + [0]
    first_core = c == 0
    first_chip = y == 0

    def copy(source, target, send, recv, device):
        return pltpu.make_async_remote_copy(
            src_ref=source, dst_ref=target, send_sem=send, recv_sem=recv,
            device_id={"ctx": device}, device_id_type=pl.DeviceIdType.MESH,
        )

    barrier = pltpu.get_barrier_semaphore()
    friends = [core_peer, chip_peer] + [away[step] * 4 + y * 2 + c for step in range(1, planes)]
    for friend in friends:
        pl.semaphore_signal(
            barrier, inc=1, device_id={"ctx": friend}, device_id_type=pl.DeviceIdType.MESH
        )
    pl.semaphore_wait(barrier, len(friends))

    pending = []
    core_rate = copy(
        decays.at[1 - c], core_rates, few_send.at[0], few_recv.at[0], core_peer
    )
    core_rate.start()
    pending.append(core_rate)
    sides = (1 - y, y)
    swaps = []
    for turn, side in enumerate(sides):
        swap = copy(
            own.at[1 - c, side], cores.at[side], core_send.at[turn], core_recv.at[turn], core_peer
        )
        swap.start()
        swaps.append(swap)
    pending += swaps

    def core_states(side, plane):
        here, there = own[c, side, plane].astype(F32), cores[side, plane].astype(F32)
        return jnp.where(first_core, here, there), jnp.where(first_core, there, here)

    def chip_state(side, plane):
        earlier, later = core_states(side, plane)
        rate = jnp.where(first_core, core_rates[side, plane], decays[c, side, plane])
        return rate * earlier + later

    core_rate.wait_recv()
    for plane in range(planes):
        chip_rate_out[plane] = decays[c, 1 - y, plane] * core_rates[1 - y, plane]
    chip_rate = copy(chip_rate_out, chip_rates, few_send.at[1], few_recv.at[1], chip_peer)
    chip_rate.start()
    pending.append(chip_rate)
    swaps[0].wait_recv()
    chip_copies = {}
    for step in order:
        plane = away[step]
        sent[plane] = chip_state(1 - y, plane).astype(BF16)
        chip_copies[step] = copy(
            sent.at[plane], chips.at[plane], chip_send.at[step], chip_recv.at[step], chip_peer
        )
        chip_copies[step].start()
        pending.append(chip_copies[step])
    swaps[1].wait_recv()
    for step in order:
        kept[away[step]] = chip_state(y, away[step]).astype(BF16)

    def chip_states(plane):
        here, there = kept[plane].astype(F32), chips[plane].astype(F32)
        return jnp.where(first_chip, here, there), jnp.where(first_chip, there, here)

    def chip_rate_pair(plane):
        here = decays[c, y, plane] * core_rates[y, plane]
        there = chip_rates[plane]
        return jnp.where(first_chip, here, there), jnp.where(first_chip, there, here)

    chip_rate.wait_recv()
    out_copies, rate_copies = {}, {}
    for step in order:
        plane = away[step]
        earlier, later = chip_rate_pair(plane)
        if step == 0:
            plane_rates[plane] = earlier * later
        else:
            plane_rate_out[plane] = earlier * later
            rate_copies[step] = copy(
                plane_rate_out.at[plane], plane_rates.at[z], rate_send.at[step],
                rate_recv.at[step], plane * 4 + y * 2 + c,
            )
            rate_copies[step].start()
            pending.append(rate_copies[step])
    for step in order:
        plane = away[step]
        chip_copies[step].wait_recv()
        earlier, later = chip_states(plane)
        both = (chip_rate_pair(plane)[1] * earlier + later).astype(BF16)
        if step == 0:
            plane_in[plane] = both
        else:
            plane_out[plane] = both
            out_copies[step] = copy(
                plane_out.at[plane], plane_in.at[z], out_send.at[step], out_recv.at[step],
                plane * 4 + y * 2 + c,
            )
            out_copies[step].start()
            pending.append(out_copies[step])
    for step in range(1, planes):
        out_copies[step].wait_recv()
        rate_copies[step].wait_recv()

    now = start[...]
    for plane in range(planes):
        enter[plane] = now.astype(BF16)
        now = plane_rates[plane] * now + plane_in[plane].astype(F32)
    final[...] = now
    in_copies = {}
    for step in range(1, planes):
        plane = away[step]
        in_copies[step] = copy(
            enter.at[plane], entered.at[z], in_send.at[step], in_recv.at[step],
            plane * 4 + y * 2 + c,
        )
        in_copies[step].start()
        pending.append(in_copies[step])

    hands = []

    def to_cores(side, plane, state, slot):
        earlier, _ = core_states(side, plane)
        rate = jnp.where(first_core, decays[c, side, plane], core_rates[side, plane])
        later = rate * state + earlier
        incoming[c, side, plane] = jnp.where(first_core, state, later).astype(BF16)
        handed[side, plane] = jnp.where(first_core, later, state).astype(BF16)
        hand = copy(
            handed.at[side, plane], incoming.at[c, side, plane],
            hand_send.at[slot], hand_recv.at[slot], core_peer,
        )
        hand.start()
        hands.append(hand)

    back_copies = {}
    receive_order = [0] + list(range(1, planes))
    for step in receive_order:
        plane = (z + planes - step) % planes
        if step == 0:
            state = enter[plane].astype(F32)
        else:
            in_copies[step].wait_recv()
            state = entered[plane].astype(F32)
        earlier, _ = chip_states(plane)
        later = chip_rate_pair(plane)[0] * state + earlier
        back[plane] = jnp.where(first_chip, later, state).astype(BF16)
        back_copies[step] = copy(
            back.at[plane], mixed.at[plane], back_send.at[step], back_recv.at[step], chip_peer
        )
        back_copies[step].start()
        pending.append(back_copies[step])
        to_cores(y, plane, jnp.where(first_chip, state, later), step)
    for step in receive_order:
        plane = (z + planes - step) % planes
        back_copies[step].wait_recv()
        to_cores(1 - y, plane, mixed[plane].astype(F32), planes + step)
    for hand in hands:
        hand.wait_recv()
    for item in pending + hands:
        item.wait_send()


def finish_kernel(partial, act_c, incoming, grown, expand, gain, out, summed):
    share = incoming.shape[-1]
    dests = out.shape[1] // share
    squares = jnp.zeros((partial.shape[0], 1), F32)
    for dest in range(dests):
        at = slice(dest * share, (dest + 1) * share)
        wide = jnp.dot(grown[0], expand[:, at], preferred_element_type=F32)
        off = jnp.dot(
            act_c[...], incoming[dest % 2, dest // 2 % 2, dest // 4], preferred_element_type=F32
        )
        total = partial[:, at].astype(F32) + wide * off
        summed[:, at] = total
        squares = squares + jnp.sum(total * total, axis=1, keepdims=True)
    factor = lax.rsqrt(squares * (1.0 / out.shape[1]) + 1e-05)
    for dest in range(dests):
        at = slice(dest * share, (dest + 1) * share)
        out[:, at] = (summed[:, at] * factor * gain[:, at]).astype(BF16)


def shards(xbc, conv_carry, conv_weight, step_size, decay, skip_gain, norm_gain, init_state):
    taps, channels = conv_weight.shape
    rows = xbc.shape[0]
    heads = step_size.shape[1]
    inner = heads * P_SIZE
    count = lax.axis_size("ctx")
    position = lax.axis_index("ctx")
    share = inner // count
    head_share = heads // count
    width = inner // GROUPS
    per_group = heads // GROUPS
    dests = width // share

    edge = xbc[rows - (taps - 1) :]
    received = lax.ppermute(edge, "ctx", [(s, s + 1) for s in range(count - 1)])
    earlier = jnp.where(position == 0, conv_carry, received).astype(F32)
    earlier = jnp.pad(earlier, ((8 - (taps - 1), 0), (0, 0)))

    vmem = pl.BlockSpec(memory_space=pltpu.VMEM)
    pairs = jax.ShapeDtypeStruct((GROUPS, rows, 2 * per_group), BF16)
    factor, grown, cum_rows, shifted, skips = pl.pallas_call(
        prepare_kernel,
        in_specs=[vmem] * 3,
        out_specs=[vmem] * 5,
        out_shape=[
            pairs,
            pairs,
            jax.ShapeDtypeStruct((GROUPS, rows, per_group), F32),
            jax.ShapeDtypeStruct((heads, rows), F32),
            jax.ShapeDtypeStruct((GROUPS, 16, 2 * per_group), BF16),
        ],
        name="prepare",
    )(decay, step_size, skip_gain[None])
    spread = np.repeat(np.eye(per_group, dtype=np.float32), P_SIZE, axis=1)
    expand = jnp.asarray(np.concatenate([spread, spread], axis=0), BF16)
    planes = count // 4

    def wide(height):
        return pl.BlockSpec((height, width), lambda g: (0, g))

    def thin(height, first):
        return pl.BlockSpec((height, N), lambda g: (0, first + g))

    def per(*shape):
        return pl.BlockSpec((1,) + shape, lambda g: (g, 0, 0))

    whole_expand = pl.BlockSpec((2 * per_group, width), lambda g: (0, 0))
    piece = pl.BlockSpec((2, 2, dests // 4, N, share), lambda g: (0, 0, g, 0, 0))
    b_first, c_first = inner // N, inner // N + GROUPS
    rate = pl.BlockSpec((2, 2, dests // 4, 1, share), lambda g: (0, 0, g, 0, 0))
    act_c, own, decays, partial = pl.pallas_call(
        conv_kernel,
        grid=(GROUPS,),
        in_specs=[
            wide(rows), thin(rows, b_first), thin(rows, c_first),
            wide(8), thin(8, b_first), thin(8, c_first),
            wide(taps), thin(taps, b_first), thin(taps, c_first),
            per(rows, 2 * per_group), per(rows, 2 * per_group), per(rows, per_group),
            pl.BlockSpec((per_group, rows), lambda g: (g, 0)), per(16, 2 * per_group),
            whole_expand,
        ],
        out_specs=[thin(rows, 0), piece, rate, wide(rows)],
        out_shape=[
            jax.ShapeDtypeStruct((rows, GROUPS * N), BF16),
            jax.ShapeDtypeStruct((2, 2, planes, N, share), BF16),
            jax.ShapeDtypeStruct((2, 2, planes, 1, share), F32),
            jax.ShapeDtypeStruct((rows, inner), BF16),
        ],
        scratch_shapes=[
            pltpu.VMEM((8 + rows, LANES), F32),
            pltpu.VMEM((rows, width), BF16),
            pltpu.VMEM((rows, N), BF16),
        ],
        compiler_params=params(),
        name="conv_state",
    )(xbc, xbc, xbc, earlier, earlier, earlier, conv_weight, conv_weight, conv_weight, factor, grown,
      cum_rows, shifted, skips, expand)

    start = lax.dynamic_slice_in_dim(init_state, position * head_share, head_share, 0)
    start = start.astype(F32).reshape(share, N).T
    line = pltpu.VMEM((planes, N, share), BF16)
    square = pltpu.VMEM((2, planes, N, share), BF16)
    turns = pltpu.SemaphoreType.DMA((planes,))
    incoming, final = pl.pallas_call(
        functools.partial(scan_kernel, planes),
        in_specs=[vmem] * 3,
        out_specs=[vmem] * 2,
        out_shape=[
            jax.ShapeDtypeStruct((2, 2, planes, N, share), BF16),
            jax.ShapeDtypeStruct((N, share), F32),
        ],
        scratch_shapes=[square] + [line] * 9 + [square]
        + [pltpu.VMEM((2, planes, 1, share), F32)] + [pltpu.VMEM((planes, 1, share), F32)] * 4
        + [pltpu.SemaphoreType.DMA((2,))] * 2 + [turns] * 10
        + [pltpu.SemaphoreType.DMA((2 * planes,))] * 2 + [pltpu.SemaphoreType.DMA((2,))] * 2,
        compiler_params=pltpu.CompilerParams(
            collective_id=0, has_side_effects=True, vmem_limit_bytes=VMEM_LIMIT
        ),
        name="scan_devices",
    )(own, decays, start)
    final_state = final.T.reshape(head_share, P_SIZE, N)

    mixed_out = pl.pallas_call(
        finish_kernel,
        grid=(GROUPS,),
        in_specs=[
            wide(rows), thin(rows, 0), piece, per(rows, 2 * per_group), whole_expand, wide(1),
        ],
        out_specs=wide(rows),
        out_shape=jax.ShapeDtypeStruct((rows, inner), BF16),
        scratch_shapes=[pltpu.VMEM((rows, width), F32)],
        compiler_params=params(),
        name="finish",
    )(partial, act_c, incoming, grown, expand, norm_gain[None])
    return (mixed_out, final_state)


def solution(mesh):
    return jax.shard_map(
        shards,
        mesh=mesh,
        in_specs=(
            P(("groups", "ctx"), None),
            P("groups", None),
            P(),
            P(("groups", "ctx"), None),
            P(("groups", "ctx"), None),
            P(),
            P(),
            P("groups", None, None),
        ),
        out_specs=(P(("groups", "ctx"), None), P(("groups", "ctx"), None, None)),
        check_vma=False,
    )
```

```python
import functools

import jax
import jax.numpy as jnp
import numpy as np
from jax import lax
from jax.experimental import pallas as pl
from jax.experimental.pallas import tpu as pltpu
from jax.sharding import PartitionSpec as P

P_SIZE = 64
N = 128
GROUPS = 4
LANES = 128
F32 = jnp.float32
BF16 = jnp.bfloat16
VMEM_LIMIT = 48 * 1024 * 1024


def params():
    return pltpu.CompilerParams(
        dimension_semantics=("arbitrary",), vmem_limit_bytes=VMEM_LIMIT
    )


def split_bf16(value):
    high = value.astype(BF16)
    low = (value - high.astype(F32)).astype(BF16)
    return high, low


def prepare(decay, step, skip, factor, grown, cum_rows, shifted, skips):
    rows, heads = decay.shape
    row_index = lax.broadcasted_iota(jnp.int32, (rows, rows), 0)
    col_index = lax.broadcasted_iota(jnp.int32, (rows, rows), 1)
    lower = jnp.where(row_index >= col_index, 1.0, 0.0).astype(F32)
    cum = jnp.dot(
        lower, jnp.log2(decay[...]), precision=lax.Precision.HIGHEST, preferred_element_type=F32
    )
    per_group = heads // GROUPS
    shifted[...] = (cum - jnp.log2(step[...])).T.reshape(GROUPS, per_group, rows)

    def doubled(value, out):
        high, low = split_bf16(value)
        for group in range(GROUPS):
            at = slice(group * per_group, (group + 1) * per_group)
            out[group] = jnp.concatenate([high[:, at], low[:, at]], axis=1)

    doubled(jnp.exp2(cum[rows - 1 :] - cum) * step[...], factor)
    doubled(jnp.exp2(cum), grown)
    doubled(jnp.broadcast_to(skip[...], (16, heads)), skips)
    for group in range(GROUPS):
        cum_rows[group] = cum[:, group * per_group : (group + 1) * per_group]


def conv_columns(x_ref, early_ref, weight_ref, out_ref, padded, rows):
    def column(index, _):
        at = pl.ds(pl.multiple_of(index * LANES, LANES), LANES)
        padded[0:8, :] = early_ref[:, at]
        padded[8 : 8 + rows, :] = x_ref[:, at].astype(F32)
        taps = weight_ref[:, at]
        summed = taps[0:1] * padded[5 : 5 + rows, :]
        for tap in range(1, 4):
            summed = summed + taps[tap : tap + 1] * padded[5 + tap : 5 + tap + rows, :]
        half = 0.5 * summed
        out_ref[:, at] = (half * jnp.tanh(half) + half).astype(BF16)
        return 0

    lax.fori_loop(0, x_ref.shape[1] // LANES, column, 0)


def conv_kernel(
    xv, xb, xc, ev, eb, ec, wv, wb, wc, decay, step, skip, expand,
    act_c, state, decays, partial, all_grown, padded, act_v, act_b,
    all_factor, all_cum, all_shifted, all_skips
):
    group = pl.program_id(0)

    @pl.when(group == 0)
    def _():
        prepare(decay, step, skip, all_factor, all_grown, all_cum, all_shifted, all_skips)

    own = pl.ds(group, 1)
    factor, grown, cum_rows = all_factor.at[own], all_grown.at[own], all_cum.at[own]
    shifted, skips = all_shifted.at[own], all_skips.at[own]
    rows = xv.shape[0]
    conv_columns(xv, ev, wv, act_v, padded, rows)
    conv_columns(xb, eb, wb, act_b, padded, rows)
    conv_columns(xc, ec, wc, act_c, padded, rows)
    b_turned = act_b[...].astype(F32).T.astype(BF16)
    share = state.shape[-1]
    dests = xv.shape[1] // share
    for dest in range(dests):
        at = slice(dest * share, (dest + 1) * share)
        wide = jnp.dot(factor[0], expand[:, at], preferred_element_type=F32)
        scaled = (act_v[:, at].astype(F32) * wide).astype(BF16)
        state[dest % 2, dest // 2 % 2, dest // 4] = jnp.dot(b_turned, scaled, preferred_element_type=F32).astype(BF16)
        lasting = jnp.dot(grown[0, rows - 16 :], expand[:, at], preferred_element_type=F32)
        decays[dest % 2, dest // 2 % 2, dest // 4] = lasting[15:16]
    diag_part(act_v, act_b, act_c, cum_rows, shifted, skips, expand, partial)


def diag_part(act_v, act_b, act_c, cum_rows, shifted, skips, expand, partial):
    rows = act_v.shape[0]
    half = rows // 2
    heads = cum_rows.shape[2]
    scores = lax.dot_general(
        act_c[...], act_b[...], (((1,), (1,)), ((), ())), preferred_element_type=F32
    )
    row_index = lax.broadcasted_iota(jnp.int32, (half, half), 0)
    col_index = lax.broadcasted_iota(jnp.int32, (half, half), 1)
    lower = row_index >= col_index
    first_lanes = lax.broadcasted_iota(jnp.int32, (half, 2 * P_SIZE), 1) < P_SIZE
    cum = cum_rows[0]
    for pair in range(heads // 2):
        at = slice(pair * 2 * P_SIZE, (pair + 1) * 2 * P_SIZE)
        values = act_v[:, at]
        tops, lows = [], []
        for head in (2 * pair, 2 * pair + 1):
            own = cum[:, head : head + 1]
            other = shifted[0, head : head + 1, :]
            top = jnp.where(lower, own[:half] - other[:, :half], -1e30)
            w_top = (scores[:half, :half] * jnp.exp2(top)).astype(BF16)
            left = own[half:] - other[:, :half]
            w_left = (scores[half:, :half] * jnp.exp2(left)).astype(BF16)
            right = jnp.where(lower, own[half:] - other[:, half:], -1e30)
            w_right = (scores[half:, half:] * jnp.exp2(right)).astype(BF16)
            tops.append(jnp.dot(w_top, values[:half], preferred_element_type=F32))
            w_low = jnp.concatenate([w_left, w_right], axis=1)
            lows.append(jnp.dot(w_low, values, preferred_element_type=F32))
        gain = jnp.dot(skips[0], expand[:, at], preferred_element_type=F32)[0:1]
        wide = values.astype(F32)
        partial[:half, at] = (
            jnp.where(first_lanes, tops[0], tops[1]) + gain * wide[:half]
        ).astype(BF16)
        partial[half:, at] = (
            jnp.where(first_lanes, lows[0], lows[1]) + gain * wide[half:]
        ).astype(BF16)


def scan_kernel(
    planes, own, decays, start, incoming, final,
    cores, sent, kept, chips, plane_out, plane_in, enter, entered, back, mixed, handed,
    core_rates, chip_rate_out, chip_rates, plane_rate_out, plane_rates,
    core_send, core_recv, chip_send, chip_recv, out_send, out_recv,
    in_send, in_recv, back_send, back_recv, rate_send, rate_recv,
    hand_send, hand_recv, few_send, few_recv,
):
    position = lax.axis_index("ctx")
    z, y, c = position // 4, (position // 2) % 2, position % 2
    core_peer = position + 1 - 2 * c
    chip_peer = position + 2 - 4 * y
    away = [(z + step) % planes for step in range(planes)]
    order = list(range(1, planes)) + [0]
    first_core = c == 0
    first_chip = y == 0

    def copy(source, target, send, recv, device):
        return pltpu.make_async_remote_copy(
            src_ref=source, dst_ref=target, send_sem=send, recv_sem=recv,
            device_id={"ctx": device}, device_id_type=pl.DeviceIdType.MESH,
        )

    barrier = pltpu.get_barrier_semaphore()
    friends = [core_peer, chip_peer] + [away[step] * 4 + y * 2 + c for step in range(1, planes)]
    for friend in friends:
        pl.semaphore_signal(
            barrier, inc=1, device_id={"ctx": friend}, device_id_type=pl.DeviceIdType.MESH
        )
    pl.semaphore_wait(barrier, len(friends))

    pending = []
    core_rate = copy(
        decays.at[1 - c], core_rates, few_send.at[0], few_recv.at[0], core_peer
    )
    core_rate.start()
    pending.append(core_rate)
    sides = (1 - y, y)
    swaps = []
    for turn, side in enumerate(sides):
        swap = copy(
            own.at[1 - c, side], cores.at[side], core_send.at[turn], core_recv.at[turn], core_peer
        )
        swap.start()
        swaps.append(swap)
    pending += swaps

    def core_states(side, plane):
        here, there = own[c, side, plane].astype(F32), cores[side, plane].astype(F32)
        return jnp.where(first_core, here, there), jnp.where(first_core, there, here)

    def chip_state(side, plane):
        earlier, later = core_states(side, plane)
        rate = jnp.where(first_core, core_rates[side, plane], decays[c, side, plane])
        return rate * earlier + later

    core_rate.wait_recv()
    for plane in range(planes):
        chip_rate_out[plane] = decays[c, 1 - y, plane] * core_rates[1 - y, plane]
    chip_rate = copy(chip_rate_out, chip_rates, few_send.at[1], few_recv.at[1], chip_peer)
    chip_rate.start()
    pending.append(chip_rate)
    swaps[0].wait_recv()
    chip_copies = {}
    for step in order:
        plane = away[step]
        sent[plane] = chip_state(1 - y, plane).astype(BF16)
        chip_copies[step] = copy(
            sent.at[plane], chips.at[plane], chip_send.at[step], chip_recv.at[step], chip_peer
        )
        chip_copies[step].start()
        pending.append(chip_copies[step])
    swaps[1].wait_recv()
    for step in order:
        kept[away[step]] = chip_state(y, away[step]).astype(BF16)

    def chip_states(plane):
        here, there = kept[plane].astype(F32), chips[plane].astype(F32)
        return jnp.where(first_chip, here, there), jnp.where(first_chip, there, here)

    def chip_rate_pair(plane):
        here = decays[c, y, plane] * core_rates[y, plane]
        there = chip_rates[plane]
        return jnp.where(first_chip, here, there), jnp.where(first_chip, there, here)

    chip_rate.wait_recv()
    out_copies, rate_copies = {}, {}
    for step in order:
        plane = away[step]
        earlier, later = chip_rate_pair(plane)
        if step == 0:
            plane_rates[plane] = earlier * later
        else:
            plane_rate_out[plane] = earlier * later
            rate_copies[step] = copy(
                plane_rate_out.at[plane], plane_rates.at[z], rate_send.at[step],
                rate_recv.at[step], plane * 4 + y * 2 + c,
            )
            rate_copies[step].start()
            pending.append(rate_copies[step])
    for step in order:
        plane = away[step]
        chip_copies[step].wait_recv()
        earlier, later = chip_states(plane)
        both = (chip_rate_pair(plane)[1] * earlier + later).astype(BF16)
        if step == 0:
            plane_in[plane] = both
        else:
            plane_out[plane] = both
            out_copies[step] = copy(
                plane_out.at[plane], plane_in.at[z], out_send.at[step], out_recv.at[step],
                plane * 4 + y * 2 + c,
            )
            out_copies[step].start()
            pending.append(out_copies[step])
    for step in range(1, planes):
        out_copies[step].wait_recv()
        rate_copies[step].wait_recv()

    now = start[...]
    for plane in range(planes):
        enter[plane] = now.astype(BF16)
        now = plane_rates[plane] * now + plane_in[plane].astype(F32)
    final[...] = now
    in_copies = {}
    for step in range(1, planes):
        plane = away[step]
        in_copies[step] = copy(
            enter.at[plane], entered.at[z], in_send.at[step], in_recv.at[step],
            plane * 4 + y * 2 + c,
        )
        in_copies[step].start()
        pending.append(in_copies[step])

    hands = []

    def to_cores(side, plane, state, slot):
        earlier, _ = core_states(side, plane)
        rate = jnp.where(first_core, decays[c, side, plane], core_rates[side, plane])
        later = rate * state + earlier
        incoming[c, side, plane] = jnp.where(first_core, state, later).astype(BF16)
        handed[side, plane] = jnp.where(first_core, later, state).astype(BF16)
        hand = copy(
            handed.at[side, plane], incoming.at[c, side, plane],
            hand_send.at[slot], hand_recv.at[slot], core_peer,
        )
        hand.start()
        hands.append(hand)

    back_copies = {}
    receive_order = [0] + list(range(1, planes))
    for step in receive_order:
        plane = (z + planes - step) % planes
        if step == 0:
            state = enter[plane].astype(F32)
        else:
            in_copies[step].wait_recv()
            state = entered[plane].astype(F32)
        earlier, _ = chip_states(plane)
        later = chip_rate_pair(plane)[0] * state + earlier
        back[plane] = jnp.where(first_chip, later, state).astype(BF16)
        back_copies[step] = copy(
            back.at[plane], mixed.at[plane], back_send.at[step], back_recv.at[step], chip_peer
        )
        back_copies[step].start()
        pending.append(back_copies[step])
        to_cores(y, plane, jnp.where(first_chip, state, later), step)
    for step in receive_order:
        plane = (z + planes - step) % planes
        back_copies[step].wait_recv()
        to_cores(1 - y, plane, mixed[plane].astype(F32), planes + step)
    for hand in hands:
        hand.wait_recv()
    for item in pending + hands:
        item.wait_send()


def finish_kernel(partial, act_c, incoming, grown, expand, gain, out, summed):
    share = incoming.shape[-1]
    dests = out.shape[1] // share
    squares = jnp.zeros((partial.shape[0], 1), F32)
    for dest in range(dests):
        at = slice(dest * share, (dest + 1) * share)
        wide = jnp.dot(grown[0], expand[:, at], preferred_element_type=F32)
        off = jnp.dot(
            act_c[...], incoming[dest % 2, dest // 2 % 2, dest // 4], preferred_element_type=F32
        )
        total = partial[:, at].astype(F32) + wide * off
        summed[:, at] = total
        squares = squares + jnp.sum(total * total, axis=1, keepdims=True)
    factor = lax.rsqrt(squares * (1.0 / out.shape[1]) + 1e-05)
    for dest in range(dests):
        at = slice(dest * share, (dest + 1) * share)
        out[:, at] = (summed[:, at] * factor * gain[:, at]).astype(BF16)


def shards(xbc, conv_carry, conv_weight, step_size, decay, skip_gain, norm_gain, init_state):
    taps, channels = conv_weight.shape
    rows = xbc.shape[0]
    heads = step_size.shape[1]
    inner = heads * P_SIZE
    count = lax.axis_size("ctx")
    position = lax.axis_index("ctx")
    share = inner // count
    head_share = heads // count
    width = inner // GROUPS
    per_group = heads // GROUPS
    dests = width // share

    edge = xbc[rows - (taps - 1) :]
    received = lax.ppermute(edge, "ctx", [(s, s + 1) for s in range(count - 1)])
    earlier = jnp.where(position == 0, conv_carry, received).astype(F32)
    earlier = jnp.pad(earlier, ((8 - (taps - 1), 0), (0, 0)))

    vmem = pl.BlockSpec(memory_space=pltpu.VMEM)
    spread = np.repeat(np.eye(per_group, dtype=np.float32), P_SIZE, axis=1)
    expand = jnp.asarray(np.concatenate([spread, spread], axis=0), BF16)
    planes = count // 4

    def wide(height):
        return pl.BlockSpec((height, width), lambda g: (0, g))

    def thin(height, first):
        return pl.BlockSpec((height, N), lambda g: (0, first + g))

    def per(*shape):
        return pl.BlockSpec((1,) + shape, lambda g: (g, 0, 0))

    def fixed(*shape):
        return pl.BlockSpec(shape, lambda g: (0,) * len(shape))

    pairs = (GROUPS, rows, 2 * per_group)
    whole_expand = pl.BlockSpec((2 * per_group, width), lambda g: (0, 0))
    piece = pl.BlockSpec((2, 2, dests // 4, N, share), lambda g: (0, 0, g, 0, 0))
    b_first, c_first = inner // N, inner // N + GROUPS
    rate = pl.BlockSpec((2, 2, dests // 4, 1, share), lambda g: (0, 0, g, 0, 0))
    act_c, own, decays, partial, grown = pl.pallas_call(
        conv_kernel,
        grid=(GROUPS,),
        in_specs=[
            wide(rows), thin(rows, b_first), thin(rows, c_first),
            wide(8), thin(8, b_first), thin(8, c_first),
            wide(taps), thin(taps, b_first), thin(taps, c_first),
            fixed(rows, heads), fixed(rows, heads), fixed(1, heads), whole_expand,
        ],
        out_specs=[thin(rows, 0), piece, rate, wide(rows), fixed(*pairs)],
        out_shape=[
            jax.ShapeDtypeStruct((rows, GROUPS * N), BF16),
            jax.ShapeDtypeStruct((2, 2, planes, N, share), BF16),
            jax.ShapeDtypeStruct((2, 2, planes, 1, share), F32),
            jax.ShapeDtypeStruct((rows, inner), BF16),
            jax.ShapeDtypeStruct(pairs, BF16),
        ],
        scratch_shapes=[
            pltpu.VMEM((8 + rows, LANES), F32),
            pltpu.VMEM((rows, width), BF16),
            pltpu.VMEM((rows, N), BF16),
            pltpu.VMEM(pairs, BF16),
            pltpu.VMEM((GROUPS, rows, per_group), F32),
            pltpu.VMEM((GROUPS, per_group, rows), F32),
            pltpu.VMEM((GROUPS, 16, 2 * per_group), BF16),
        ],
        compiler_params=params(),
        name="conv_state",
    )(xbc, xbc, xbc, earlier, earlier, earlier, conv_weight, conv_weight, conv_weight, decay,
      step_size, skip_gain[None], expand)

    start = lax.dynamic_slice_in_dim(init_state, position * head_share, head_share, 0)
    start = start.astype(F32).reshape(share, N).T
    line = pltpu.VMEM((planes, N, share), BF16)
    square = pltpu.VMEM((2, planes, N, share), BF16)
    turns = pltpu.SemaphoreType.DMA((planes,))
    incoming, final = pl.pallas_call(
        functools.partial(scan_kernel, planes),
        in_specs=[vmem] * 3,
        out_specs=[vmem] * 2,
        out_shape=[
            jax.ShapeDtypeStruct((2, 2, planes, N, share), BF16),
            jax.ShapeDtypeStruct((N, share), F32),
        ],
        scratch_shapes=[square] + [line] * 9 + [square]
        + [pltpu.VMEM((2, planes, 1, share), F32)] + [pltpu.VMEM((planes, 1, share), F32)] * 4
        + [pltpu.SemaphoreType.DMA((2,))] * 2 + [turns] * 10
        + [pltpu.SemaphoreType.DMA((2 * planes,))] * 2 + [pltpu.SemaphoreType.DMA((2,))] * 2,
        compiler_params=pltpu.CompilerParams(
            collective_id=0, has_side_effects=True, vmem_limit_bytes=VMEM_LIMIT
        ),
        name="scan_devices",
    )(own, decays, start)
    final_state = final.T.reshape(head_share, P_SIZE, N)

    mixed_out = pl.pallas_call(
        finish_kernel,
        grid=(GROUPS,),
        in_specs=[
            wide(rows), thin(rows, 0), piece, per(rows, 2 * per_group), whole_expand, wide(1),
        ],
        out_specs=wide(rows),
        out_shape=jax.ShapeDtypeStruct((rows, inner), BF16),
        scratch_shapes=[pltpu.VMEM((rows, width), F32)],
        compiler_params=params(),
        name="finish",
    )(partial, act_c, incoming, grown, expand, norm_gain[None])
    return (mixed_out, final_state)


def solution(mesh):
    return jax.shard_map(
        shards,
        mesh=mesh,
        in_specs=(
            P(("groups", "ctx"), None),
            P("groups", None),
            P(),
            P(("groups", "ctx"), None),
            P(("groups", "ctx"), None),
            P(),
            P(),
            P("groups", None, None),
        ),
        out_specs=(P(("groups", "ctx"), None), P(("groups", "ctx"), None, None)),
        check_vma=False,
    )
```
